128 devices in a mesh: dp: 8 (over x_lo, z), tile: 16 (over x_hi, y, core).
Axes of the slice: x: 4 (x_hi: 2, x_lo: 2; x = x_hi * 2 + x_lo), y: 4, z: 4, core: 2. Of those that a mesh axis runs over, the one named last changes fastest.
Arguments:
- gradient: bfloat16 [9216, 7168], P('dp', 'tile'), may hold values from -0.1875 to 0.1875
- stats_old: float32 [7168, 7168], P('dp', 'tile'), as said below
- owner_map: int32 [8, 16], P('dp'), may hold values from 0 to 15, as said below
Outputs:
- refreshed: float32 [7168, 7168], P('dp', 'tile')
- owned_rows: float32 [256, 56, 7168], P(('dp', 'tile'))
The draws below stay inside these ranges and needn't reach their ends.
Inputs may be any that keep to these rules, and one draw needn't show every extreme that they name: `owner_map`: in each row group no tile index owns more than 2 row units, and some tile index owns exactly 2. `stats_old`: Symmetric.
All inputs are finite; a program needn't handle non-finite values.
Results may differ from the reference program's by a relative error of at most 0.0003.
Values may be sent and summed in bfloat16 or wider, within the bound.
A program may use at most 192 MiB of HBM per device.

```python
import jax
import jax.numpy as jnp
from jax import lax

D = 7168
CAP = 2
HID = 9216
ROWS_DP = 1152
RB = 56
N_DP = 8
N_TILE = 16


def draw_stats_old(key, part):
    key = jax.random.fold_in(key, 3)
    key_jitter, key_scales = jax.random.split(key)
    jitter = jax.random.normal(key_jitter, (D, D), jnp.float32)
    scales = jnp.exp(jax.random.uniform(key_scales, (D,), jnp.float32, 0.0, 2.3))
    position = jnp.arange(D)
    diagonal = jnp.where(position[:, None] == position[None, :], scales[None, :], 0.0)
    return 0.03 * (jitter + jitter.T) + diagonal


def draw_owner_map(key, part):
    key = jax.random.fold_in(key, 7)
    quarter = jnp.arange(N_TILE) * 4 // N_TILE
    counts = jnp.array([2, 1, 1, 0], jnp.int32)[quarter]
    listing = []
    for group in range(N_DP):
        key_group = jax.random.fold_in(key, group)
        key_labels, key_order = jax.random.split(key_group)
        labels = jax.random.permutation(key_labels, N_TILE)
        owners = jnp.repeat(labels, counts, total_repeat_length=N_TILE)
        listing.append(jax.random.permutation(key_order, owners))
    return jnp.stack(listing).astype(jnp.int32)


def steps_of(own_key, dims, cuts, low, largest):
    level = 1.0
    for axis_at, blocks in cuts:
        draws = jax.random.uniform(jax.random.fold_in(jax.random.fold_in(own_key, 6), axis_at), (blocks,), jnp.float32, low / len(cuts), largest / len(cuts))
        level = level * jnp.repeat(jnp.exp(draws), dims[axis_at] // blocks).reshape((-1,) + (1,) * (len(dims) - 1 - axis_at))
    return level


def normal_values(rng, dims, width, limit, shards=(), kind=jnp.bfloat16):
    level = steps_of(rng, dims, shards, -0.22, 0.18) if shards else 1.0
    values = jax.random.normal(rng, dims, jnp.float32) * width * level
    return jnp.minimum(jnp.maximum(values, -limit), limit).astype(kind)


def setup_inputs(seed: int = 0) -> dict:
    splits = jax.random.split(jax.random.key(seed), 4)
    gradient = normal_values(splits[0], (HID, D), (HID // 10) ** -0.5, 0.1875, ((0, 8), (1, 16)))
    stats_old = draw_stats_old(jax.random.fold_in(splits[3], 71), 0)
    owner_map = draw_owner_map(jax.random.fold_in(splits[3], 71), 0)
    return dict(gradient=gradient, stats_old=stats_old, owner_map=owner_map)


EMA_DECAY = 0.9


def slot_select(owners, count, slots):
    position = jnp.arange(count, dtype=jnp.int32)
    matches = owners[:, None] == owners[None, :]
    earlier = position[None, :] < position[:, None]
    ranking = jnp.sum((matches & earlier).astype(jnp.int32), axis=1)
    chosen = (owners[None, None, :] == position[None, :, None]) & (ranking[None, None, :] == jnp.arange(slots, dtype=jnp.int32)[:, None, None])
    return chosen.astype(jnp.float32)


def reference(gradient, stats_old, owner_map):
    summed = jnp.zeros((D, D), jnp.float32)
    for group in range(N_DP):
        piece = gradient[group * ROWS_DP:(group + 1) * ROWS_DP]
        partial_value = lax.dot_general(piece, piece, (((0,), (0,)), ((), ())), preferred_element_type=jnp.float32)
        summed = summed + partial_value
    refreshed = EMA_DECAY * stats_old + (1.0 - EMA_DECAY) * summed
    unit_rows = refreshed.reshape(N_DP, N_TILE, RB, D)
    selection = jax.vmap(lambda owners: slot_select(owners, N_TILE, CAP))(owner_map)
    owned = jnp.einsum("gseu,gurc->gesrc", selection, unit_rows, precision=lax.Precision.HIGHEST)
    return refreshed, owned.reshape(N_DP * N_TILE * CAP, RB, D)
```

```python
import functools

import jax
import jax.numpy as jnp
from jax import lax
from jax.experimental import pallas as pl
from jax.experimental.pallas import tpu as pltpu
from jax.sharding import PartitionSpec as P

MESH = pl.DeviceIdType.MESH
EMA_DECAY = 0.9
Q = 7
LEVELS = 32767.0


def kernel(grad, stats, owner, refreshed, owned, cols, rows, prod, zin, coded, out16, in16,
           c_s, c_r, b_s, b_r, y_s, y_r, f_s, f_r, k_s, k_r, z_s, z_r, o_s, o_r):
    depth, width = grad.shape
    high = width // Q
    unit = owned.shape[1]
    dp, tile = lax.axis_index("dp"), lax.axis_index("tile")
    a, z = dp // 4, dp % 4
    b, y, core = tile // 8, (tile // 2) % 4, tile % 2
    middle = a != b

    def at(a_, z_, b_, y_, core_):
        return {"dp": a_ * 4 + z_, "tile": b_ * 8 + y_ * 2 + core_}

    partner = at(1 - a, z, b, y, core)
    bridge = at(1 - a, z, 1 - b, y, core)
    sibling = at(a, z, b, y, 1 - core)
    yu, yd, yo = (y + 1) % 4, (y + 3) % 4, (y + 2) % 4
    zu, zd, zo = (z + 1) % 4, (z + 3) % 4, (z + 2) % 4
    up_y, down_y = at(a, z, b, yu, core), at(a, z, b, yd, core)
    up_z, down_z = at(a, zu, b, y, core), at(a, zd, b, y, core)

    def copy(src, dst, send, recv, device):
        return pltpu.make_async_remote_copy(
            src_ref=src, dst_ref=dst, send_sem=send, recv_sem=recv, device_id=device, device_id_type=MESH
        )

    def c_copy(q, p):
        part = cols.at[p, pl.ds(q * high, high)]
        return copy(part, part, c_s.at[q], c_r.at[q], partner)

    def b_copy(q, p, which):
        return copy(cols.at[p, pl.ds(q * high, high)], rows.at[q, core, y, p], b_s.at[q, which], b_r.at[q, which], bridge)

    def y_copy(q, which):
        part = rows.at[q, core, y]
        return copy(part, part, y_s.at[q, which], y_r.at[q, which], up_y if which else down_y)

    def y_arrived(q, which):
        part = rows.at[q, core, yd if which else yu]
        return copy(part, part, y_s.at[q, which], y_r.at[q, which], up_y if which else down_y)

    def f_copy(q, which):
        part = rows.at[q, core, yd if which else yu, which]
        return copy(part, part, f_s.at[q, which], f_r.at[q, which], up_y if which else down_y)

    def f_arrived(q, which):
        part = rows.at[q, core, yo, which]
        return copy(part, part, f_s.at[q, which], f_r.at[q, which], up_y if which else down_y)

    def k_copy(q, half):
        part = rows.at[q, half]
        return copy(part, part, k_s.at[q], k_r.at[q], sibling)

    def z_copy(q, slot):
        half, dest, device = {
            0: (0, zu, up_z), 1: (1, zu, up_z), 2: (0, zd, down_z), 3: (1, zd, down_z), 4: (1, zo, up_z), 5: (0, zo, down_z),
        }[slot]
        return copy(prod.at[q, half, dest], zin.at[q, slot], z_s.at[q, slot], z_r.at[q, slot], device)

    def o_copy(e):
        return copy(out16.at[e], in16.at[tile], o_s.at[e], o_r.at[tile], {"tile": e})

    def o_arrived(e):
        return copy(out16.at[e], in16.at[e], o_s.at[e], o_r.at[e], {"tile": e})

    barrier = pltpu.get_barrier_semaphore()

    def greet(e, _):
        @pl.when(e != tile)
        def _():
            pl.semaphore_signal(barrier, inc=1, device_id={"tile": e}, device_id_type=MESH)
        return 0

    for device in (partner, bridge, up_z, down_z):
        pl.semaphore_signal(barrier, inc=1, device_id=device, device_id_type=MESH)
    lax.fori_loop(0, 16, greet, 0)

    block = 0
    begun = False
    while block < width:
        wide = min(128, width - block)
        cols[a, block:block + wide, :] = grad[:, block:block + wide].T
        if not begun:
            pl.semaphore_wait(barrier, 19)
            begun = True
        for q in range(block // high, (block + wide) // high):
            c_copy(q, a).start()

            @pl.when(middle)
            def _(q=q):
                b_copy(q, a, 0).start()
        block += wide

    def c_step(q):
        c_copy(q, 1 - a).wait_recv()

        @pl.when(middle)
        def _():
            b_copy(q, 1 - a, 1).start()

        @pl.when(jnp.logical_not(middle))
        def _():
            for p in range(2):
                rows[q, core, y, p] = cols[p, pl.ds(pl.multiple_of(q * high, high), high), :]

    def e1(q):
        @pl.when(middle)
        def _():
            for which in range(2):
                b_copy(q, a, which).wait_recv()
        for which in range(2):
            y_copy(q, which).start()

    def e2(q):
        for which in range(2):
            y_arrived(q, which).wait_recv()
            f_copy(q, which).start()

    def e3(q):
        for which in range(2):
            f_arrived(q, which).wait_recv()
        k_copy(q, core).start()

    def e4(q):
        k_copy(q, 1 - core).wait_recv()
        for half in range(2):
            total = None
            for p in range(2):
                left = rows[q, half, :, p].reshape(4 * high, depth)
                part = lax.dot_general(left, cols[p], (((1,), (1,)), ((), ())), preferred_element_type=jnp.float32)
                total = part if total is None else total + part
            prod[q, half] = total.reshape(4, high, width)
        for slot in (4, 5, 0, 3):
            z_copy(q, slot).start()

    def e5(q):
        z_copy(q, 4).wait_recv()
        prod[q, 1, zu] += zin[q, 4]
        z_copy(q, 1).start()
        z_copy(q, 5).wait_recv()
        prod[q, 0, zd] += zin[q, 5]
        z_copy(q, 2).start()

    def e6(q):
        for slot in range(4):
            z_copy(q, slot).wait_recv()
        for half in range(2):
            place = pl.ds(pl.multiple_of(half * width + q * high, 8), high)
            summed = prod[q, half, z] + zin[q, half] + zin[q, 2 + half]
            refreshed[place, :] = EMA_DECAY * stats[place, :] + (1.0 - EMA_DECAY) * summed

    def step(i, _):
        for k in range(2):
            pl.when(2 * i + k < Q)(functools.partial(c_step, 2 * i + k))
        pl.when(i < Q)(functools.partial(e1, i))
        pl.when((i >= 1) & (i < Q + 1))(functools.partial(e2, i - 1))
        pl.when((i >= 2) & (i < Q + 2))(functools.partial(e3, i - 2))
        pl.when((i >= 3) & (i < Q + 3))(functools.partial(e5, i - 3))
        pl.when((i >= 4) & (i < Q + 4))(functools.partial(e6, i - 4))
        pl.when((i >= 2) & (i < Q + 2))(functools.partial(e4, i - 2))
        return 0

    lax.fori_loop(0, 2, step, 0)
    for q in range(4, Q):
        c_step(q)

    def late(i, _):
        pl.when(i < Q)(functools.partial(e1, i))
        pl.when(i < Q + 1)(functools.partial(e2, i - 1))
        pl.when(i < Q + 2)(functools.partial(e3, i - 2))
        pl.when((i >= 3) & (i < Q + 3))(functools.partial(e5, i - 3))
        pl.when(i >= 4)(functools.partial(e6, i - 4))
        pl.when(i < Q + 2)(functools.partial(e4, i - 2))
        return 0

    lax.fori_loop(2, Q + 4, late, 0)

    def encode(u, _):
        values = refreshed[pl.ds(pl.multiple_of(u * unit, 8), unit), :]
        for first in range(0, width, 128):
            last = min(first + 128, width)
            part = values[:, first:last]
            most = jnp.maximum(jnp.max(jnp.abs(part), axis=1, keepdims=True), 2.0 ** -100)
            power = jnp.ceil(8.0 * jnp.log2(most))
            part = jnp.clip(part * (jnp.exp2(power * -0.125) * LEVELS), -LEVELS, LEVELS)
            coded[u, :, first:last] = jnp.round(part)
            place = width + 16 * (first // 128)
            coded[u, :, place:place + 16] = jnp.broadcast_to(power, (unit, 16))
        return 0

    lax.fori_loop(0, 16, encode, 0)

    def send(j, _):
        e = (tile + 1 + j) % 16
        count, first, second = jnp.int32(0), jnp.int32(0), jnp.int32(0)
        for u in range(16):
            mine = (owner[0, u] == e).astype(jnp.int32)
            first = first + jnp.where(count == 0, mine * u, 0)
            second = second + jnp.where(count == 1, mine * u, 0)
            count = count + mine
        pieces = [coded[u] * (count > s).astype(jnp.float32) for s, u in enumerate((first, second))]
        out16[e] = jnp.concatenate(pieces, axis=0).astype(jnp.int32).astype(jnp.int16)

        @pl.when(j < 15)
        def _():
            o_copy(e).start()
        return 0

    lax.fori_loop(0, 16, send, 0)
    in16[tile] = out16[tile]

    def await_owned(j, _):
        o_arrived((tile + 15 - j) % 16).wait_recv()
        return 0

    lax.fori_loop(0, 15, await_owned, 0)
    for pair in range(8):
        parts = []
        for k in range(2):
            got = in16[2 * pair + k].astype(jnp.int32).astype(jnp.float32)
            pieces = []
            for first in range(0, width, 128):
                place = width + 16 * (first // 128)
                scale = jnp.exp2(got[:, place:place + 1] * 0.125) * (1.0 / LEVELS)
                pieces.append(got[:, first:min(first + 128, width)] * scale)
            parts.append(jnp.concatenate(pieces, axis=1))
        both = jnp.concatenate(parts, axis=1)
        for s in range(2):
            owned[s, :, pair * 2 * width:(pair + 1) * 2 * width] = both[s * unit:(s + 1) * unit]

    def drain(q, _):
        c_copy(q, a).wait_send()

        @pl.when(middle)
        def _():
            b_copy(q, a, 0).wait_send()
            b_copy(q, 1 - a, 1).wait_send()
        for which in range(2):
            y_copy(q, which).wait_send()
            f_copy(q, which).wait_send()
        k_copy(q, core).wait_send()
        for slot in range(6):
            z_copy(q, slot).wait_send()
        return 0

    lax.fori_loop(0, Q, drain, 0)

    def drain_owned(j, _):
        o_copy((tile + 1 + j) % 16).wait_send()
        return 0

    lax.fori_loop(0, 15, drain_owned, 0)


def local(gradient, stats_old, owner_map):
    depth, width = gradient.shape
    high = width // Q
    rows = stats_old.shape[0]
    unit = rows // 16
    dma = pltpu.SemaphoreType.DMA
    vmem = pl.BlockSpec(memory_space=pltpu.VMEM)
    return pl.pallas_call(
        kernel,
        out_shape=(
            jax.ShapeDtypeStruct((rows, width), jnp.float32),
            jax.ShapeDtypeStruct((2, unit, 16 * width), jnp.float32),
        ),
        in_specs=[vmem, vmem, pl.BlockSpec(memory_space=pltpu.SMEM)],
        out_specs=(vmem, vmem),
        scratch_shapes=[
            pltpu.VMEM((2, width, depth), jnp.bfloat16),
            pltpu.VMEM((Q, 2, 4, 2, high, depth), jnp.bfloat16),
            pltpu.VMEM((Q, 2, 4, high, width), jnp.float32),
            pltpu.VMEM((Q, 6, high, width), jnp.float32),
            pltpu.VMEM((16, unit, 512), jnp.float32),
            pltpu.VMEM((16, 2 * unit, 512), jnp.int16),
            pltpu.VMEM((16, 2 * unit, 512), jnp.int16),
            dma((Q,)), dma((Q,)),
            dma((Q, 2)), dma((Q, 2)),
            dma((Q, 2)), dma((Q, 2)),
            dma((Q, 2)), dma((Q, 2)),
            dma((Q,)), dma((Q,)),
            dma((Q, 6)), dma((Q, 6)),
            dma((16,)), dma((16,)),
        ],
        compiler_params=pltpu.CompilerParams(
            collective_id=0, has_side_effects=True, vmem_limit_bytes=60 << 20
        ),
    )(gradient, stats_old, owner_map)


def solution(mesh):
    return jax.shard_map(
        local,
        mesh=mesh,
        in_specs=(P("dp", "tile"), P("dp", "tile"), P("dp", None)),
        out_specs=(P("dp", "tile"), P(("dp", "tile"), None, None)),
        check_vma=False,
    )
```

```python
import functools

import jax
import jax.numpy as jnp
from jax import lax
from jax.experimental import pallas as pl
from jax.experimental.pallas import tpu as pltpu
from jax.sharding import PartitionSpec as P

MESH = pl.DeviceIdType.MESH
EMA_DECAY = 0.9
Q = 7
LEVELS = 32767.0


def encode(values, axis):
    most = jnp.maximum(jnp.max(jnp.abs(values), axis=axis, keepdims=True), 2.0 ** -100)
    power = jnp.ceil(8.0 * jnp.log2(most))
    return jnp.round(jnp.clip(values * jnp.exp2(15.0 - 0.125 * power), -LEVELS, LEVELS)), power


def step_of(power):
    return jnp.exp2(0.125 * power - 15.0)


def pack(values):
    whole, power = encode(values, 0)
    return jnp.concatenate([whole, jnp.broadcast_to(power, (16, power.shape[1]))], axis=0).astype(jnp.int32).astype(jnp.int16)


def unpack(code):
    high = code.shape[0] - 16
    code = code.astype(jnp.int32).astype(jnp.float32)
    return code[:high] * step_of(code[high:high + 1])


def kernel(grad, stats, owner, refreshed, owned, cols, rows, prod, zin, zout, coded, out16, in16,
           g_s, c_s, c_r, b_s, b_r, y_s, y_r, f_s, f_r, k_s, k_r, z_s, z_r, o_s, o_r):
    width, depth = grad.shape
    high = width // Q
    part_w = width // 2
    unit = owned.shape[1]
    dp, tile = lax.axis_index("dp"), lax.axis_index("tile")
    a, z = dp // 4, dp % 4
    b, y, core = tile // 8, (tile // 2) % 4, tile % 2
    middle = a != b

    def at(a_, z_, b_, y_, core_):
        return {"dp": a_ * 4 + z_, "tile": b_ * 8 + y_ * 2 + core_}

    partner = at(1 - a, z, b, y, core)
    bridge = at(1 - a, z, 1 - b, y, core)
    sibling = at(a, z, b, y, 1 - core)
    yu, yd, yo = (y + 1) % 4, (y + 3) % 4, (y + 2) % 4
    zu, zd, zo = (z + 1) % 4, (z + 3) % 4, (z + 2) % 4
    up_y, down_y = at(a, z, b, yu, core), at(a, z, b, yd, core)
    up_z, down_z = at(a, zu, b, y, core), at(a, zd, b, y, core)

    def copy(src, dst, send, recv, device):
        return pltpu.make_async_remote_copy(
            src_ref=src, dst_ref=dst, send_sem=send, recv_sem=recv, device_id=device, device_id_type=MESH
        )

    def c_copy(q):
        place = pl.ds(q * high, high)
        return copy(grad.at[place], cols.at[a, place], c_s.at[q], c_r.at[q], partner)

    def c_arrived(q):
        part = cols.at[1 - a, pl.ds(q * high, high)]
        return copy(part, part, c_s.at[q], c_r.at[q], partner)

    def b_copy(q, which):
        place = pl.ds(q * high, high)
        p = 1 - a if which else a
        return copy(cols.at[p, place] if which else grad.at[place], rows.at[q, core, y, p], b_s.at[q, which], b_r.at[q, which], bridge)

    def b_arrived(q, which):
        part = rows.at[q, core, y, a if which else 1 - a]
        return copy(part, part, b_s.at[q, which], b_r.at[q, which], bridge)

    def y_copy(q, which, p):
        part = rows.at[q, core, y, p]
        return copy(part, part, y_s.at[q, which, p], y_r.at[q, which, p], up_y if which else down_y)

    def y_arrived(q, which, p):
        part = rows.at[q, core, yd if which else yu, p]
        return copy(part, part, y_s.at[q, which, p], y_r.at[q, which, p], up_y if which else down_y)

    def f_copy(q, which):
        part = rows.at[q, core, yd if which else yu, which]
        return copy(part, part, f_s.at[q, which], f_r.at[q, which], up_y if which else down_y)

    def f_arrived(q, which):
        part = rows.at[q, core, yo, which]
        return copy(part, part, f_s.at[q, which], f_r.at[q, which], up_y if which else down_y)

    def k_copy(q, dest, half):
        part = rows.at[q, half, dest]
        return copy(part, part, k_s.at[q, dest], k_r.at[q, dest], sibling)

    def z_copy(q, slot):
        return copy(zout.at[q, slot], zin.at[q, slot], z_s.at[q, slot], z_r.at[q, slot], down_z if slot in (2, 3, 5) else up_z)

    def o_copy(e):
        return copy(out16.at[e], in16.at[tile], o_s.at[e], o_r.at[tile], {"tile": e})

    def o_arrived(e):
        return copy(out16.at[e], in16.at[e], o_s.at[e], o_r.at[e], {"tile": e})

    barrier = pltpu.get_barrier_semaphore()

    def greet(e, _):
        @pl.when(e != tile)
        def _():
            pl.semaphore_signal(barrier, inc=1, device_id={"tile": e}, device_id_type=MESH)
        return 0

    for device in (partner, bridge, up_z, down_z):
        pl.semaphore_signal(barrier, inc=1, device_id=device, device_id_type=MESH)
    lax.fori_loop(0, 16, greet, 0)

    own = pltpu.make_async_copy(grad, cols.at[a], g_s)
    own.start()
    pl.semaphore_wait(barrier, 19)

    def begin(q, _):
        c_copy(q).start()
        return 0

    lax.fori_loop(0, Q, begin, 0)

    @pl.when(middle)
    def _():
        b_copy(0, 0).start()
    own.wait()

    def c_step(q):
        @pl.when(middle & (q > 0))
        def _():
            b_copy(q, 0).start()
        c_arrived(q).wait_recv()

        @pl.when(middle)
        def _():
            b_copy(q, 1).start()

    def ready(q, p, which):
        @pl.when(middle)
        def _():
            b_arrived(q, which).wait_recv()

        @pl.when(jnp.logical_not(middle))
        def _():
            rows[q, core, y, p] = cols[p, pl.ds(pl.multiple_of(q * high, high), high), :]

    def e1(q, which):
        p = jnp.where(middle, 1 - a, a)
        p = 1 - p if which else p
        ready(q, p, which)
        for way in range(2):
            y_copy(q, way, p).start()
        if which:
            k_copy(q, y, core).start()

    def e2(q):
        for which in range(2):
            y_arrived(q, which, which).wait_recv()
            f_copy(q, which).start()
        for which in range(2):
            y_arrived(q, which, 1 - which).wait_recv()
        for dest in (yu, yd):
            k_copy(q, dest, core).start()

    def e3(q):
        for which in range(2):
            f_arrived(q, which).wait_recv()
        k_copy(q, yo, core).start()

    def e4(q):
        for dest in range(4):
            k_copy(q, dest, 1 - core).wait_recv()
        for first in (0, 2):
            total = None
            for p in range(2):
                right = jnp.concatenate([rows[q, half, dest, p] for dest in (first, first + 1) for half in range(2)], axis=0)
                part = lax.dot_general(cols[p], right, (((1,), (1,)), ((), ())), preferred_element_type=jnp.float32)
                total = part if total is None else total + part
            prod[q, first] = total[:, :2 * high]
            prod[q, first + 1] = total[:, 2 * high:]
        for slot, half, dest in ((4, 1, zo), (5, 0, zo), (0, 0, zu), (3, 1, zd)):
            zout[q, slot] = pack(prod[q, dest, half * part_w:(half + 1) * part_w, :])
            z_copy(q, slot).start()

    def e5(q):
        for slot, half, dest in ((1, 1, zu), (2, 0, zd)):
            z_copy(q, 3 + slot).wait_recv()
            zout[q, slot] = pack(prod[q, dest, half * part_w:(half + 1) * part_w, :] + unpack(zin[q, 3 + slot]))
            z_copy(q, slot).start()

    def e6(q):
        for slot in range(4):
            z_copy(q, slot).wait_recv()
        summed = prod[q, z] + jnp.concatenate([unpack(zin[q, k]) + unpack(zin[q, k + 2]) for k in range(2)], axis=0)
        lane = lax.broadcasted_iota(jnp.int32, (width, 2 * high), 1) // high
        places, shifts = [], []
        for half in range(2):
            at_ = half * Q + q
            places.append(pl.ds(pl.multiple_of(at_ // 2 * (2 * high), 2 * high), 2 * high))
            shifts.append((at_ + half) % 2 * high)
        old = [pltpu.roll(stats[:, places[half]], shifts[half], axis=1) for half in range(2)]
        fresh = EMA_DECAY * jnp.where(lane == 0, old[0], old[1]) + (1.0 - EMA_DECAY) * summed
        for half in range(2):
            moved = pltpu.roll(fresh, shifts[half], axis=1)
            refreshed[:, places[half]] = jnp.where(lane == (half * Q + q) % 2, moved, refreshed[:, places[half]])
        across = fresh.T
        pieces, powers = [], []
        for first in range(0, width, 128):
            part = across[:, first:min(first + 128, width)]
            whole, power = encode(part, 1)
            pieces.append(whole)
            powers.append(jnp.broadcast_to(power, (2 * high, 16)))
        code = jnp.concatenate(pieces + powers, axis=1).reshape(2, high // 8, 8, 512)
        for half in range(2):
            coded[pl.ds(half * (width // 8) + q * (high // 8), high // 8)] = code[half]

    def step(i, _):
        def at_step(first, fun):
            pl.when((i >= first) & (i < first + Q))(functools.partial(fun, i - first))

        at_step(0, functools.partial(e1, which=0))
        for k in range(2):
            pl.when(2 * i + k < Q)(functools.partial(c_step, 2 * i + k))
        at_step(0, functools.partial(e1, which=1))
        at_step(1, e2)
        pl.when(i == 4)(functools.partial(e5, 0))
        pl.when((i >= 4) & (i < Q + 3))(functools.partial(e5, i - 3))
        at_step(2, e3)

        pl.when(i == 3)(functools.partial(e4, 0))
        pl.when((i >= 3) & (i < Q + 2))(functools.partial(e4, i - 2))
        pl.when(i == 5)(functools.partial(e6, 0))
        pl.when((i >= 5) & (i < Q + 4))(functools.partial(e6, i - 4))
        return 0

    lax.fori_loop(0, Q + 4, step, 0)

    def peer(j):
        return (b + 1 - j // 8) % 2 * 8 + (y + 1 + j // 2) % 4 * 2 + (core + 1 - j % 2) % 2

    def send(j, _):
        e = peer(j)
        count, first, second = jnp.int32(0), jnp.int32(0), jnp.int32(0)
        for u in range(16):
            mine = (owner[0, u] == e).astype(jnp.int32)
            first = first + jnp.where(count == 0, mine * u, 0)
            second = second + jnp.where(count == 1, mine * u, 0)
            count = count + mine
        pieces = []
        for s, u in enumerate((first, second)):
            held = (count > s).astype(jnp.float32)
            pieces += [coded[u * (unit // 8) + k] * held for k in range(unit // 8)]
        out16[e] = jnp.concatenate(pieces, axis=0).astype(jnp.int32).astype(jnp.int16)

        @pl.when(j < 15)
        def _():
            o_copy(e).start()
        return 0

    lax.fori_loop(0, 16, send, 0)

    def decode(k, _):
        parts = []
        pair = peer(2 * k) // 2
        for c in range(2):
            e = 2 * pair + c

            @pl.when(e != tile)
            def _(e=e):
                o_arrived(e).wait_recv()

            @pl.when(e == tile)
            def _(e=e):
                in16[e] = out16[e]
            got = in16[e].astype(jnp.int32).astype(jnp.float32)
            pieces = []
            for first in range(0, width, 128):
                place = width + 16 * (first // 128)
                scale = jnp.exp2(got[:, place:place + 1] * 0.125) * (1.0 / LEVELS)
                pieces.append(got[:, first:min(first + 128, width)] * scale)
            parts.append(jnp.concatenate(pieces, axis=1))
        both = jnp.concatenate(parts, axis=1)
        for s in range(2):
            owned[s, :, pl.ds(pl.multiple_of(pair * 2 * width, 128), 2 * width)] = both[s * unit:(s + 1) * unit]
        return 0

    lax.fori_loop(0, 8, decode, 0)

    def drain(q, _):
        c_copy(q).wait_send()

        @pl.when(middle)
        def _():
            for which in range(2):
                b_copy(q, which).wait_send()
        for which in range(2):
            for p in range(2):
                y_copy(q, which, p).wait_send()
            f_copy(q, which).wait_send()
        for dest in range(4):
            k_copy(q, dest, core).wait_send()
        for slot in range(6):
            z_copy(q, slot).wait_send()
        return 0

    lax.fori_loop(0, Q, drain, 0)

    def drain_owned(j, _):
        o_copy(peer(j)).wait_send()
        return 0

    lax.fori_loop(0, 15, drain_owned, 0)


def local(gradient, stats_old, owner_map):
    depth, width = gradient.shape
    high = width // Q
    rows = stats_old.shape[0]
    unit = rows // 16
    dma = pltpu.SemaphoreType.DMA
    vmem = pl.BlockSpec(memory_space=pltpu.VMEM)
    refreshed, owned = pl.pallas_call(
        kernel,
        out_shape=(
            jax.ShapeDtypeStruct((width, rows), jnp.float32),
            jax.ShapeDtypeStruct((2, unit, 16 * width), jnp.float32),
        ),
        in_specs=[pl.BlockSpec(memory_space=pl.ANY), vmem, pl.BlockSpec(memory_space=pltpu.SMEM)],
        out_specs=(vmem, vmem),
        scratch_shapes=[
            pltpu.VMEM((2, width, depth), jnp.bfloat16),
            pltpu.VMEM((Q, 2, 4, 2, high, depth), jnp.bfloat16),
            pltpu.VMEM((Q, 4, width, 2 * high), jnp.float32),
            pltpu.VMEM((Q, 6, width // 2 + 16, 2 * high), jnp.int16),
            pltpu.VMEM((Q, 6, width // 2 + 16, 2 * high), jnp.int16),
            pltpu.VMEM((rows // 8, 8, 512), jnp.float32),
            pltpu.VMEM((16, 2 * unit, 512), jnp.int16),
            pltpu.VMEM((16, 2 * unit, 512), jnp.int16),
            dma,
            dma((Q,)), dma((Q,)),
            dma((Q, 2)), dma((Q, 2)),
            dma((Q, 2, 2)), dma((Q, 2, 2)),
            dma((Q, 2)), dma((Q, 2)),
            dma((Q, 4)), dma((Q, 4)),
            dma((Q, 6)), dma((Q, 6)),
            dma((16,)), dma((16,)),
        ],
        compiler_params=pltpu.CompilerParams(
            collective_id=0, has_side_effects=True, vmem_limit_bytes=60 << 20
        ),
    )(gradient.T, stats_old.T, owner_map)
    return refreshed.T, owned


def solution(mesh):
    return jax.shard_map(
        local,
        mesh=mesh,
        in_specs=(P("dp", "tile"), P("dp", "tile"), P("dp", None)),
        out_specs=(P("dp", "tile"), P(("dp", "tile"), None, None)),
        check_vma=False,
    )
```

```python
import functools

import jax
import jax.numpy as jnp
from jax import lax
from jax.experimental import pallas as pl
from jax.experimental.pallas import tpu as pltpu
from jax.sharding import PartitionSpec as P

MESH = pl.DeviceIdType.MESH
EMA_DECAY = 0.9
Q = 7
STEPS = 2
LEVELS = 32767.0


def encode(values, axis):
    most = jnp.maximum(jnp.max(jnp.abs(values), axis=axis, keepdims=True), 2.0 ** -100)
    power = jnp.ceil(8.0 * jnp.log2(most))
    return jnp.round(jnp.clip(values * jnp.exp2(15.0 - 0.125 * power), -LEVELS, LEVELS)), power


def step_of(power):
    return jnp.exp2(0.125 * power - 15.0)


def pack(values):
    whole, power = encode(values, 0)
    return jnp.concatenate([whole, jnp.broadcast_to(power, (16, power.shape[1]))], axis=0).astype(jnp.int32).astype(jnp.int16)


def unpack(code):
    high = code.shape[0] - 16
    code = code.astype(jnp.int32).astype(jnp.float32)
    return code[:high] * step_of(code[high:high + 1])


def kernel(grad, stats_in, owner, refreshed_out, in16, cols, rows, stats, refreshed, prod, zin, zout, coded, out16,
           g_s, t_s, w_s, m_s, c_s, c_r, b_s, b_r, y_s, y_r, f_s, f_r, k_s, k_r, z_s, z_r, o_s, o_r):
    width, depth = grad.shape
    high = width // Q
    part_w = width // 2
    unit = in16.shape[1] // 2
    dp, tile = lax.axis_index("dp"), lax.axis_index("tile")
    a, z = dp // 4, dp % 4
    b, y, core = tile // 8, (tile // 2) % 4, tile % 2
    middle = a != b

    def at(a_, z_, b_, y_, core_):
        return {"dp": a_ * 4 + z_, "tile": b_ * 8 + y_ * 2 + core_}

    partner = at(1 - a, z, b, y, core)
    bridge = at(1 - a, z, 1 - b, y, core)
    sibling = at(a, z, b, y, 1 - core)
    yu, yd, yo = (y + 1) % 4, (y + 3) % 4, (y + 2) % 4
    zu, zd, zo = (z + 1) % 4, (z + 3) % 4, (z + 2) % 4
    up_y, down_y = at(a, z, b, yu, core), at(a, z, b, yd, core)
    up_z, down_z = at(a, zu, b, y, core), at(a, zd, b, y, core)

    def copy(src, dst, send, recv, device):
        return pltpu.make_async_remote_copy(
            src_ref=src, dst_ref=dst, send_sem=send, recv_sem=recv, device_id=device, device_id_type=MESH
        )

    def c_copy(q):
        place = pl.ds(q * high, high)
        return copy(grad.at[place], cols.at[a, place], c_s.at[q], c_r.at[q], partner)

    def c_arrived(q):
        part = cols.at[1 - a, pl.ds(q * high, high)]
        return copy(part, part, c_s.at[q], c_r.at[q], partner)

    def b_copy(q, which):
        place = pl.ds(q * high, high)
        p = 1 - a if which else a
        return copy(cols.at[p, place] if which else grad.at[place], rows.at[q, core, y, p], b_s.at[q, which], b_r.at[q, which], bridge)

    def b_arrived(q, which):
        part = rows.at[q, core, y, a if which else 1 - a]
        return copy(part, part, b_s.at[q, which], b_r.at[q, which], bridge)

    def y_copy(q, which, p):
        part = rows.at[q, core, y, p]
        return copy(part, part, y_s.at[q, which, p], y_r.at[q, which, p], up_y if which else down_y)

    def y_arrived(q, which, p):
        part = rows.at[q, core, yd if which else yu, p]
        return copy(part, part, y_s.at[q, which, p], y_r.at[q, which, p], up_y if which else down_y)

    def f_copy(q, which):
        part = rows.at[q, core, yd if which else yu, which]
        return copy(part, part, f_s.at[q, which], f_r.at[q, which], up_y if which else down_y)

    def f_arrived(q, which):
        part = rows.at[q, core, yo, which]
        return copy(part, part, f_s.at[q, which], f_r.at[q, which], up_y if which else down_y)

    def k_copy(q, dest, half):
        part = rows.at[q, half, dest]
        return copy(part, part, k_s.at[q, dest], k_r.at[q, dest], sibling)

    def z_copy(q, slot):
        return copy(zout.at[q, slot], zin.at[q, slot], z_s.at[q, slot], z_r.at[q, slot], down_z if slot in (2, 3, 5) else up_z)

    def o_copy(e):
        return copy(out16.at[e], in16.at[tile], o_s.at[e], o_r.at[tile], {"tile": e})

    def o_arrived(e):
        return copy(out16.at[e], in16.at[e], o_s.at[e], o_r.at[e], {"tile": e})

    barrier = pltpu.get_barrier_semaphore()

    def greet(e, _):
        @pl.when(e != tile)
        def _():
            pl.semaphore_signal(barrier, inc=1, device_id={"tile": e}, device_id_type=MESH)
        return 0

    for device in (partner, bridge, up_z, down_z):
        pl.semaphore_signal(barrier, inc=1, device_id=device, device_id_type=MESH)
    lax.fori_loop(0, 16, greet, 0)

    own = pltpu.make_async_copy(grad, cols.at[a], g_s)
    own.start()
    old_stats = pltpu.make_async_copy(stats_in, stats, t_s)
    old_stats.start()
    pl.semaphore_wait(barrier, 19)

    def begin(q, _):
        c_copy(q).start()
        return 0

    @pl.when(middle)
    def _():
        b_copy(0, 0).start()
    lax.fori_loop(0, Q, begin, 0)
    own.wait()

    def c_step(q):
        @pl.when(middle & (q > 0))
        def _():
            b_copy(q, 0).start()
        c_arrived(q).wait_recv()

        @pl.when(middle)
        def _():
            b_copy(q, 1).start()

    def ready(q, p, which):
        @pl.when(middle)
        def _():
            b_arrived(q, which).wait_recv()

        @pl.when(jnp.logical_not(middle))
        def _():
            rows[q, core, y, p] = cols[p, pl.ds(pl.multiple_of(q * high, high), high), :]

    def e1(q, which):
        p = jnp.where(middle, 1 - a, a)
        p = 1 - p if which else p
        ready(q, p, which)
        for way in range(2):
            y_copy(q, way, p).start()
        if which:
            k_copy(q, y, core).start()

    def e2(q):
        for which in range(2):
            y_arrived(q, which, which).wait_recv()
            f_copy(q, which).start()
        for which in range(2):
            y_arrived(q, which, 1 - which).wait_recv()
        for dest in (yu, yd):
            k_copy(q, dest, core).start()

    def e3(q):
        for which in range(2):
            f_arrived(q, which).wait_recv()
        k_copy(q, yo, core).start()

    def e4(q):
        for dest in range(4):
            k_copy(q, dest, 1 - core).wait_recv()
        for first in (0, 2):
            total = None
            for p in range(2):
                right = jnp.concatenate([rows[q, half, dest, p] for dest in (first, first + 1) for half in range(2)], axis=0)
                part = lax.dot_general(cols[p], right, (((1,), (1,)), ((), ())), preferred_element_type=jnp.float32)
                total = part if total is None else total + part
            prod[q, first] = total[:, :2 * high]
            prod[q, first + 1] = total[:, 2 * high:]
        for slot, half, dest in ((4, 1, zo), (5, 0, zo), (0, 0, zu), (3, 1, zd)):
            zout[q, slot] = pack(prod[q, dest, half * part_w:(half + 1) * part_w, :])
            z_copy(q, slot).start()

    def e5(q):
        for slot, half, dest in ((1, 1, zu), (2, 0, zd)):
            z_copy(q, 3 + slot).wait_recv()
            zout[q, slot] = pack(prod[q, dest, half * part_w:(half + 1) * part_w, :] + unpack(zin[q, 3 + slot]))
            z_copy(q, slot).start()

    def e6(q):
        for slot in range(4):
            z_copy(q, slot).wait_recv()
        summed = prod[q, z] + jnp.concatenate([unpack(zin[q, k]) + unpack(zin[q, k + 2]) for k in range(2)], axis=0)
        lane = lax.broadcasted_iota(jnp.int32, (width, 2 * high), 1) // high
        places, shifts = [], []
        for half in range(2):
            at_ = half * Q + q
            places.append(pl.ds(pl.multiple_of(at_ // 2 * (2 * high), 2 * high), 2 * high))
            shifts.append((at_ + half) % 2 * high)
        old = [pltpu.roll(stats[:, places[half]], shifts[half], axis=1) for half in range(2)]
        fresh = EMA_DECAY * jnp.where(lane == 0, old[0], old[1]) + (1.0 - EMA_DECAY) * summed
        for half in range(2):
            moved = pltpu.roll(fresh, shifts[half], axis=1)
            refreshed[:, places[half]] = jnp.where(lane == (half * Q + q) % 2, moved, refreshed[:, places[half]])
        across = fresh.T
        pieces, powers = [], []
        for first in range(0, width, 128):
            part = across[:, first:min(first + 128, width)]
            whole, power = encode(part, 1)
            pieces.append(whole)
            powers.append(jnp.broadcast_to(power, (2 * high, 16)))
        code = jnp.concatenate(pieces + powers, axis=1).reshape(2, high // 8, 8, 512)
        for half in range(2):
            coded[pl.ds(half * (width // 8) + q * (high // 8), high // 8)] = code[half]

    def step(i, _):
        def at_step(first, fun):
            pl.when((i >= first) & (i < first + Q))(functools.partial(fun, i - first))

        at_step(0, functools.partial(e1, which=0))
        for k in range(2):
            pl.when(2 * i + k < Q)(functools.partial(c_step, 2 * i + k))
        at_step(0, functools.partial(e1, which=1))
        at_step(1, e2)
        at_step(2, e3)
        pl.when(i == 3)(functools.partial(e4, 0))
        pl.when((i >= 3) & (i < Q + 2))(functools.partial(e4, i - 2))
        pl.when(i == 4)(functools.partial(e5, 0))
        pl.when((i >= 4) & (i < Q + 3))(functools.partial(e5, i - 3))
        pl.when(i == 4)(old_stats.wait)
        pl.when(i == 5)(functools.partial(e6, 0))
        pl.when((i >= 5) & (i < Q + 4))(functools.partial(e6, i - 4))
        return 0

    lax.fori_loop(0, Q + 4, step, 0)

    done = pltpu.make_async_copy(refreshed, refreshed_out, w_s)
    done.start()

    def peer(j):
        return (b + 1 - j // 8) % 2 * 8 + (y + 1 + j // 2) % 4 * 2 + (core + 1 - j % 2) % 2

    def send(j, _):
        e = peer(j)
        count, first, second = jnp.int32(0), jnp.int32(0), jnp.int32(0)
        for u in range(16):
            mine = (owner[0, u] == e).astype(jnp.int32)
            first = first + jnp.where(count == 0, mine * u, 0)
            second = second + jnp.where(count == 1, mine * u, 0)
            count = count + mine
        pieces = []
        for s, u in enumerate((first, second)):
            held = (count > s).astype(jnp.float32)
            pieces += [coded[u * (unit // 8) + k] * held for k in range(unit // 8)]
        out16[e] = jnp.concatenate(pieces, axis=0).astype(jnp.int32).astype(jnp.int16)

        @pl.when(j < 15)
        def _():
            o_copy(e).start()
        return 0

    lax.fori_loop(0, 16, send, 0)

    kept = pltpu.make_async_copy(out16.at[tile], in16.at[tile], m_s)
    kept.start()

    def arrive(j, _):
        o_arrived(peer(j)).wait_recv()
        return 0

    lax.fori_loop(0, 15, arrive, 0)
    kept.wait()
    done.wait()

    def drain(q, _):
        c_copy(q).wait_send()

        @pl.when(middle)
        def _():
            for which in range(2):
                b_copy(q, which).wait_send()
        for which in range(2):
            for p in range(2):
                y_copy(q, which, p).wait_send()
            f_copy(q, which).wait_send()
        for dest in range(4):
            k_copy(q, dest, core).wait_send()
        for slot in range(6):
            z_copy(q, slot).wait_send()
        return 0

    lax.fori_loop(0, Q, drain, 0)

    def drain_owned(j, _):
        o_copy(peer(j)).wait_send()
        return 0

    lax.fori_loop(0, 15, drain_owned, 0)


def finish(refreshed, in16, refreshed_out, owned):
    refreshed_out[...] = refreshed[...]
    unit = owned.shape[1]
    tiles = 16 // STEPS
    width = owned.shape[2] // tiles
    parts = []
    for c in range(tiles):
        got = in16[c].astype(jnp.int32).astype(jnp.float32)
        pieces = []
        for first in range(0, width, 128):
            place = width + 16 * (first // 128)
            pieces.append(got[:, first:min(first + 128, width)] * step_of(got[:, place:place + 1]))
        parts.append(jnp.concatenate(pieces, axis=1))
    both = jnp.concatenate(parts, axis=1)
    for s in range(2):
        owned[s] = both[s * unit:(s + 1) * unit]


def local(gradient, stats_old, owner_map):
    depth, width = gradient.shape
    high = width // Q
    rows = stats_old.shape[0]
    unit = rows // 16
    dma = pltpu.SemaphoreType.DMA
    hbm = pl.BlockSpec(memory_space=pl.ANY)
    refreshed, in16 = pl.pallas_call(
        kernel,
        out_shape=(
            jax.ShapeDtypeStruct((width, rows), jnp.float32),
            jax.ShapeDtypeStruct((16, 2 * unit, 512), jnp.int16),
        ),
        in_specs=[hbm, hbm, pl.BlockSpec(memory_space=pltpu.SMEM)],
        out_specs=(hbm, hbm),
        scratch_shapes=[
            pltpu.VMEM((2, width, depth), jnp.bfloat16),
            pltpu.VMEM((Q, 2, 4, 2, high, depth), jnp.bfloat16),
            pltpu.VMEM((width, rows), jnp.float32),
            pltpu.VMEM((width, rows), jnp.float32),
            pltpu.VMEM((Q, 4, width, 2 * high), jnp.float32),
            pltpu.VMEM((Q, 6, width // 2 + 16, 2 * high), jnp.int16),
            pltpu.VMEM((Q, 6, width // 2 + 16, 2 * high), jnp.int16),
            pltpu.VMEM((rows // 8, 8, 512), jnp.float32),
            pltpu.VMEM((16, 2 * unit, 512), jnp.int16),
            dma, dma, dma, dma,
            dma((Q,)), dma((Q,)),
            dma((Q, 2)), dma((Q, 2)),
            dma((Q, 2, 2)), dma((Q, 2, 2)),
            dma((Q, 2)), dma((Q, 2)),
            dma((Q, 4)), dma((Q, 4)),
            dma((Q, 6)), dma((Q, 6)),
            dma((16,)), dma((16,)),
        ],
        compiler_params=pltpu.CompilerParams(
            collective_id=0, has_side_effects=True, vmem_limit_bytes=60 << 20
        ),
    )(gradient.T, stats_old.T, owner_map)
    refreshed, owned = pl.pallas_call(
        finish,
        grid=(STEPS,),
        out_shape=(
            jax.ShapeDtypeStruct((width, rows), jnp.float32),
            jax.ShapeDtypeStruct((2, unit, 16 * width), jnp.float32),
        ),
        in_specs=[
            pl.BlockSpec((width // STEPS, rows), lambda i: (i, 0)),
            pl.BlockSpec((16 // STEPS, 2 * unit, 512), lambda i: (i, 0, 0)),
        ],
        out_specs=(
            pl.BlockSpec((width // STEPS, rows), lambda i: (i, 0)),
            pl.BlockSpec((2, unit, 16 // STEPS * width), lambda i: (0, 0, i)),
        ),
        compiler_params=pltpu.CompilerParams(vmem_limit_bytes=60 << 20),
    )(refreshed, in16)
    return refreshed.T, owned


def solution(mesh):
    return jax.shard_map(
        local,
        mesh=mesh,
        in_specs=(P("dp", "tile"), P("dp", "tile"), P("dp", None)),
        out_specs=(P("dp", "tile"), P(("dp", "tile"), None, None)),
        check_vma=False,
    )
```

```python
import functools

import jax
import jax.numpy as jnp
from jax import lax
from jax.experimental import pallas as pl
from jax.experimental.pallas import tpu as pltpu
from jax.sharding import PartitionSpec as P

MESH = pl.DeviceIdType.MESH
EMA_DECAY = 0.9
Q = 7
STEPS = 2
LEVELS = 32767.0


def encode(values, axis):
    most = jnp.maximum(jnp.max(jnp.abs(values), axis=axis, keepdims=True), 2.0 ** -100)
    power = jnp.ceil(8.0 * jnp.log2(most))
    return jnp.round(jnp.clip(values * jnp.exp2(15.0 - 0.125 * power), -LEVELS, LEVELS)), power


def step_of(power):
    return jnp.exp2(0.125 * power - 15.0)


def pack(values):
    whole, power = encode(values, 0)
    return jnp.concatenate([whole, jnp.broadcast_to(power, (16, power.shape[1]))], axis=0).astype(jnp.int32).astype(jnp.int16)


def unpack(code):
    high = code.shape[0] - 16
    code = code.astype(jnp.int32).astype(jnp.float32)
    return code[:high] * step_of(code[high:high + 1])


def kernel(grad, stats_in, owner, refreshed_out, in16, cols, rows, stats, refreshed, prod, zin, zout, coded, out16,
           g_s, t_s, w_s, m_s, c_s, c_r, b_s, b_r, y_s, y_r, f_s, f_r, k_s, k_r, z_s, z_r, o_s, o_r):
    width, depth = grad.shape
    high = width // Q
    part_w = width // 2
    unit = in16.shape[1] // 2
    dp, tile = lax.axis_index("dp"), lax.axis_index("tile")
    a, z = dp // 4, dp % 4
    b, y, core = tile // 8, (tile // 2) % 4, tile % 2
    middle = a != b

    def at(a_, z_, b_, y_, core_):
        return {"dp": a_ * 4 + z_, "tile": b_ * 8 + y_ * 2 + core_}

    partner = at(1 - a, z, b, y, core)
    bridge = at(1 - a, z, 1 - b, y, core)
    sibling = at(a, z, b, y, 1 - core)
    yu, yd, yo = (y + 1) % 4, (y + 3) % 4, (y + 2) % 4
    zu, zd, zo = (z + 1) % 4, (z + 3) % 4, (z + 2) % 4
    up_y, down_y = at(a, z, b, yu, core), at(a, z, b, yd, core)
    up_z, down_z = at(a, zu, b, y, core), at(a, zd, b, y, core)

    def copy(src, dst, send, recv, device):
        return pltpu.make_async_remote_copy(
            src_ref=src, dst_ref=dst, send_sem=send, recv_sem=recv, device_id=device, device_id_type=MESH
        )

    def c_copy(q):
        place = pl.ds(q * high, high)
        return copy(grad.at[place], cols.at[a, place], c_s.at[q], c_r.at[q], partner)

    def c_arrived(q):
        part = cols.at[1 - a, pl.ds(q * high, high)]
        return copy(part, part, c_s.at[q], c_r.at[q], partner)

    def b_copy(q, which):
        place = pl.ds(q * high, high)
        p = 1 - a if which else a
        return copy(cols.at[p, place] if which else grad.at[place], rows.at[q, core, y, p], b_s.at[q, which], b_r.at[q, which], bridge)

    def b_arrived(q, which):
        part = rows.at[q, core, y, a if which else 1 - a]
        return copy(part, part, b_s.at[q, which], b_r.at[q, which], bridge)

    def y_copy(q, which, p):
        part = rows.at[q, core, y, p]
        return copy(part, part, y_s.at[q, which, p], y_r.at[q, which, p], up_y if which else down_y)

    def y_arrived(q, which, p):
        part = rows.at[q, core, yd if which else yu, p]
        return copy(part, part, y_s.at[q, which, p], y_r.at[q, which, p], up_y if which else down_y)

    def f_copy(q, which):
        part = rows.at[q, core, yd if which else yu, which]
        return copy(part, part, f_s.at[q, which], f_r.at[q, which], up_y if which else down_y)

    def f_arrived(q, which):
        part = rows.at[q, core, yo, which]
        return copy(part, part, f_s.at[q, which], f_r.at[q, which], up_y if which else down_y)

    def k_copy(q, dest, half):
        part = rows.at[q, half, dest]
        return copy(part, part, k_s.at[q, dest], k_r.at[q, dest], sibling)

    def z_copy(q, slot):
        return copy(zout.at[q, slot], zin.at[q, slot], z_s.at[q, slot], z_r.at[q, slot], down_z if slot in (2, 3, 5) else up_z)

    def o_copy(e):
        return copy(out16.at[e], in16.at[tile], o_s.at[e], o_r.at[tile], {"tile": e})

    def o_arrived(e):
        return copy(out16.at[e], in16.at[e], o_s.at[e], o_r.at[e], {"tile": e})

    barrier = pltpu.get_barrier_semaphore()

    def greet(e, _):
        @pl.when(e != tile)
        def _():
            pl.semaphore_signal(barrier, inc=1, device_id={"tile": e}, device_id_type=MESH)
        return 0

    for device in (partner, bridge, up_z, down_z):
        pl.semaphore_signal(barrier, inc=1, device_id=device, device_id_type=MESH)
    lax.fori_loop(0, 16, greet, 0)

    own = pltpu.make_async_copy(grad, cols.at[a], g_s)
    own.start()
    old_stats = pltpu.make_async_copy(stats_in, stats, t_s)
    old_stats.start()
    pl.semaphore_wait(barrier, 19)

    def begin(q, _):
        c_copy(q).start()
        return 0

    @pl.when(middle)
    def _():
        b_copy(0, 0).start()
    lax.fori_loop(0, Q, begin, 0)
    own.wait()

    def c_step(q):
        @pl.when(middle & (q > 0))
        def _():
            b_copy(q, 0).start()
        c_arrived(q).wait_recv()

        @pl.when(middle)
        def _():
            b_copy(q, 1).start()

    def ready(q, p, which):
        @pl.when(middle)
        def _():
            b_arrived(q, which).wait_recv()

        @pl.when(jnp.logical_not(middle))
        def _():
            rows[q, core, y, p] = cols[p, pl.ds(pl.multiple_of(q * high, high), high), :]

    def e1(q, which):
        p = jnp.where(middle, 1 - a, a)
        p = 1 - p if which else p
        ready(q, p, which)
        for way in range(2):
            y_copy(q, way, p).start()
        if which:
            k_copy(q, y, core).start()

    def e2(q):
        for which in range(2):
            y_arrived(q, which, which).wait_recv()
            f_copy(q, which).start()
        for which in range(2):
            y_arrived(q, which, 1 - which).wait_recv()
        for dest in (yu, yd):
            k_copy(q, dest, core).start()

    def e3(q):
        for which in range(2):
            f_arrived(q, which).wait_recv()
        k_copy(q, yo, core).start()

    def product(q, dest):
        k_copy(q, dest, 1 - core).wait_recv()
        total = None
        for p in range(2):
            right = jnp.concatenate([rows[q, half, dest, p] for half in range(2)], axis=0)
            part = lax.dot_general(cols[p], right, (((1,), (1,)), ((), ())), preferred_element_type=jnp.float32)
            total = part if total is None else total + part
        prod[q, dest] = total
        for slot, half, goal in ((4, 1, zo), (5, 0, zo), (0, 0, zu), (3, 1, zd)):
            @pl.when(dest == goal)
            def _(slot=slot, half=half):
                zout[q, slot] = pack(total[half * part_w:(half + 1) * part_w])
                z_copy(q, slot).start()

    def e4a(q):
        def one(k, _):
            product(q, jnp.where(k == 0, y, jnp.where(k == 1, yu, yd)))
            return 0

        lax.fori_loop(0, 3, one, 0)

    def e4b(q):
        product(q, yo)

    def e5(q):
        for slot, half, dest in ((1, 1, zu), (2, 0, zd)):
            z_copy(q, 3 + slot).wait_recv()
            zout[q, slot] = pack(prod[q, dest, half * part_w:(half + 1) * part_w, :] + unpack(zin[q, 3 + slot]))
            z_copy(q, slot).start()

    def e6(q):
        for slot in range(4):
            z_copy(q, slot).wait_recv()
        summed = prod[q, z] + jnp.concatenate([unpack(zin[q, k]) + unpack(zin[q, k + 2]) for k in range(2)], axis=0)
        lane = lax.broadcasted_iota(jnp.int32, (width, 2 * high), 1) // high
        places, shifts = [], []
        for half in range(2):
            at_ = half * Q + q
            places.append(pl.ds(pl.multiple_of(at_ // 2 * (2 * high), 2 * high), 2 * high))
            shifts.append((at_ + half) % 2 * high)
        old = [pltpu.roll(stats[:, places[half]], shifts[half], axis=1) for half in range(2)]
        fresh = EMA_DECAY * jnp.where(lane == 0, old[0], old[1]) + (1.0 - EMA_DECAY) * summed
        for half in range(2):
            moved = pltpu.roll(fresh, shifts[half], axis=1)
            refreshed[:, places[half]] = jnp.where(lane == (half * Q + q) % 2, moved, refreshed[:, places[half]])
        across = fresh.T
        pieces, powers = [], []
        for first in range(0, width, 128):
            part = across[:, first:min(first + 128, width)]
            whole, power = encode(part, 1)
            pieces.append(whole)
            powers.append(jnp.broadcast_to(power, (2 * high, 16)))
        code = jnp.concatenate(pieces + powers, axis=1).reshape(2, high // 8, 8, 512)
        for half in range(2):
            coded[pl.ds(half * (width // 8) + q * (high // 8), high // 8)] = code[half]

    def step(i, _):
        def at_step(first, fun):
            pl.when((i >= first) & (i < first + Q))(functools.partial(fun, i - first))

        at_step(0, functools.partial(e1, which=0))
        for k in range(2):
            pl.when(2 * i + k < Q)(functools.partial(c_step, 2 * i + k))
        at_step(0, functools.partial(e1, which=1))
        at_step(1, e2)
        pl.when(i == 3)(functools.partial(e4a, 0))
        pl.when(i == 3)(functools.partial(e4b, 0))
        pl.when((i >= 3) & (i < Q + 2))(functools.partial(e4a, i - 2))
        at_step(2, e3)
        pl.when((i >= 3) & (i < Q + 2))(functools.partial(e4b, i - 2))
        pl.when(i == 4)(functools.partial(e5, 0))
        pl.when((i >= 4) & (i < Q + 3))(functools.partial(e5, i - 3))
        pl.when(i == 4)(old_stats.wait)
        pl.when(i == 5)(functools.partial(e6, 0))
        pl.when((i >= 5) & (i < Q + 4))(functools.partial(e6, i - 4))
        return 0

    lax.fori_loop(0, Q + 4, step, 0)

    done = pltpu.make_async_copy(refreshed, refreshed_out, w_s)
    done.start()

    def peer(j):
        return (b + 1 - j // 8) % 2 * 8 + (y + 1 + j // 2) % 4 * 2 + (core + 1 - j % 2) % 2

    def send(j, _):
        e = peer(j)
        count, first, second = jnp.int32(0), jnp.int32(0), jnp.int32(0)
        for u in range(16):
            mine = (owner[0, u] == e).astype(jnp.int32)
            first = first + jnp.where(count == 0, mine * u, 0)
            second = second + jnp.where(count == 1, mine * u, 0)
            count = count + mine
        pieces = []
        for s, u in enumerate((first, second)):
            held = (count > s).astype(jnp.float32)
            pieces += [coded[u * (unit // 8) + k] * held for k in range(unit // 8)]
        out16[e] = jnp.concatenate(pieces, axis=0).astype(jnp.int32).astype(jnp.int16)

        @pl.when(j < 15)
        def _():
            o_copy(e).start()
        return 0

    lax.fori_loop(0, 16, send, 0)

    kept = pltpu.make_async_copy(out16.at[tile], in16.at[tile], m_s)
    kept.start()

    def arrive(j, _):
        o_arrived(peer(j)).wait_recv()
        return 0

    lax.fori_loop(0, 15, arrive, 0)
    kept.wait()
    done.wait()

    def drain(q, _):
        c_copy(q).wait_send()

        @pl.when(middle)
        def _():
            for which in range(2):
                b_copy(q, which).wait_send()
        for which in range(2):
            for p in range(2):
                y_copy(q, which, p).wait_send()
            f_copy(q, which).wait_send()
        for dest in range(4):
            k_copy(q, dest, core).wait_send()
        for slot in range(6):
            z_copy(q, slot).wait_send()
        return 0

    lax.fori_loop(0, Q, drain, 0)

    def drain_owned(j, _):
        o_copy(peer(j)).wait_send()
        return 0

    lax.fori_loop(0, 15, drain_owned, 0)


def finish(refreshed, in16, refreshed_out, owned):
    refreshed_out[...] = refreshed[...]
    unit = owned.shape[1]
    tiles = 16 // STEPS
    width = owned.shape[2] // tiles
    parts = []
    for c in range(tiles):
        got = in16[c].astype(jnp.int32).astype(jnp.float32)
        pieces = []
        for first in range(0, width, 128):
            place = width + 16 * (first // 128)
            pieces.append(got[:, first:min(first + 128, width)] * step_of(got[:, place:place + 1]))
        parts.append(jnp.concatenate(pieces, axis=1))
    both = jnp.concatenate(parts, axis=1)
    for s in range(2):
        owned[s] = both[s * unit:(s + 1) * unit]


def local(gradient, stats_old, owner_map):
    depth, width = gradient.shape
    high = width // Q
    rows = stats_old.shape[0]
    unit = rows // 16
    dma = pltpu.SemaphoreType.DMA
    hbm = pl.BlockSpec(memory_space=pl.ANY)
    refreshed, in16 = pl.pallas_call(
        kernel,
        out_shape=(
            jax.ShapeDtypeStruct((width, rows), jnp.float32),
            jax.ShapeDtypeStruct((16, 2 * unit, 512), jnp.int16),
        ),
        in_specs=[hbm, hbm, pl.BlockSpec(memory_space=pltpu.SMEM)],
        out_specs=(hbm, hbm),
        scratch_shapes=[
            pltpu.VMEM((2, width, depth), jnp.bfloat16),
            pltpu.VMEM((Q, 2, 4, 2, high, depth), jnp.bfloat16),
            pltpu.VMEM((width, rows), jnp.float32),
            pltpu.VMEM((width, rows), jnp.float32),
            pltpu.VMEM((Q, 4, width, 2 * high), jnp.float32),
            pltpu.VMEM((Q, 6, width // 2 + 16, 2 * high), jnp.int16),
            pltpu.VMEM((Q, 6, width // 2 + 16, 2 * high), jnp.int16),
            pltpu.VMEM((rows // 8, 8, 512), jnp.float32),
            pltpu.VMEM((16, 2 * unit, 512), jnp.int16),
            dma, dma, dma, dma,
            dma((Q,)), dma((Q,)),
            dma((Q, 2)), dma((Q, 2)),
            dma((Q, 2, 2)), dma((Q, 2, 2)),
            dma((Q, 2)), dma((Q, 2)),
            dma((Q, 4)), dma((Q, 4)),
            dma((Q, 6)), dma((Q, 6)),
            dma((16,)), dma((16,)),
        ],
        compiler_params=pltpu.CompilerParams(
            collective_id=0, has_side_effects=True, vmem_limit_bytes=60 << 20
        ),
    )(gradient.T, stats_old.T, owner_map)
    refreshed, owned = pl.pallas_call(
        finish,
        grid=(STEPS,),
        out_shape=(
            jax.ShapeDtypeStruct((width, rows), jnp.float32),
            jax.ShapeDtypeStruct((2, unit, 16 * width), jnp.float32),
        ),
        in_specs=[
            pl.BlockSpec((width // STEPS, rows), lambda i: (i, 0)),
            pl.BlockSpec((16 // STEPS, 2 * unit, 512), lambda i: (i, 0, 0)),
        ],
        out_specs=(
            pl.BlockSpec((width // STEPS, rows), lambda i: (i, 0)),
            pl.BlockSpec((2, unit, 16 // STEPS * width), lambda i: (0, 0, i)),
        ),
        compiler_params=pltpu.CompilerParams(vmem_limit_bytes=60 << 20),
    )(refreshed, in16)
    return refreshed.T, owned


def solution(mesh):
    return jax.shard_map(
        local,
        mesh=mesh,
        in_specs=(P("dp", "tile"), P("dp", "tile"), P("dp", None)),
        out_specs=(P("dp", "tile"), P(("dp", "tile"), None, None)),
        check_vma=False,
    )
```

```python
import functools

import jax
import jax.numpy as jnp
from jax import lax
from jax.experimental import pallas as pl
from jax.experimental.pallas import tpu as pltpu
from jax.sharding import PartitionSpec as P

MESH = pl.DeviceIdType.MESH
EMA_DECAY = 0.9
Q = 7
STEPS = 2
LEVELS = 32767.0


def encode(values, axis):
    most = jnp.maximum(jnp.max(jnp.abs(values), axis=axis, keepdims=True), 2.0 ** -100)
    power = jnp.ceil(8.0 * jnp.log2(most))
    return jnp.round(jnp.clip(values * jnp.exp2(15.0 - 0.125 * power), -LEVELS, LEVELS)), power


def step_of(power):
    return jnp.exp2(0.125 * power - 15.0)


def pack(values):
    whole, power = encode(values, 0)
    return jnp.concatenate([whole, jnp.broadcast_to(power, (16, power.shape[1]))], axis=0).astype(jnp.int32).astype(jnp.int16)


def unpack(code):
    high = code.shape[0] - 16
    code = code.astype(jnp.int32).astype(jnp.float32)
    return code[:high] * step_of(code[high:high + 1])


def kernel(grad, stats_in, owner, refreshed_out, in16, cols, rows, stats, refreshed, prod, zin, zout, coded, out16,
           g_s, t_s, w_s, m_s, c_s, c_r, b_s, b_r, y_s, y_r, f_s, f_r, k_s, k_r, z_s, z_r, o_s, o_r):
    width, depth = grad.shape
    high = width // Q
    part_w = width // 2
    unit = 8 * coded.shape[0] // 16
    dp, tile = lax.axis_index("dp"), lax.axis_index("tile")
    a, z = dp // 4, dp % 4
    b, y, core = tile // 8, (tile // 2) % 4, tile % 2
    middle = a != b

    def at(a_, z_, b_, y_, core_):
        return {"dp": a_ * 4 + z_, "tile": b_ * 8 + y_ * 2 + core_}

    partner = at(1 - a, z, b, y, core)
    bridge = at(1 - a, z, 1 - b, y, core)
    sibling = at(a, z, b, y, 1 - core)
    yu, yd, yo = (y + 1) % 4, (y + 3) % 4, (y + 2) % 4
    zu, zd, zo = (z + 1) % 4, (z + 3) % 4, (z + 2) % 4
    up_y, down_y = at(a, z, b, yu, core), at(a, z, b, yd, core)
    up_z, down_z = at(a, zu, b, y, core), at(a, zd, b, y, core)

    def copy(src, dst, send, recv, device):
        return pltpu.make_async_remote_copy(
            src_ref=src, dst_ref=dst, send_sem=send, recv_sem=recv, device_id=device, device_id_type=MESH
        )

    def c_copy(q):
        place = pl.ds(q * high, high)
        return copy(grad.at[place], cols.at[a, place], c_s.at[q], c_r.at[q], partner)

    def c_arrived(q):
        part = cols.at[1 - a, pl.ds(q * high, high)]
        return copy(part, part, c_s.at[q], c_r.at[q], partner)

    def b_copy(q, which):
        place = pl.ds(q * high, high)
        p = 1 - a if which else a
        return copy(cols.at[p, place] if which else grad.at[place], rows.at[q, core, y, p], b_s.at[q, which], b_r.at[q, which], bridge)

    def b_arrived(q, which):
        part = rows.at[q, core, y, a if which else 1 - a]
        return copy(part, part, b_s.at[q, which], b_r.at[q, which], bridge)

    def y_copy(q, which, p):
        part = rows.at[q, core, y, p]
        return copy(part, part, y_s.at[q, which, p], y_r.at[q, which, p], up_y if which else down_y)

    def y_arrived(q, which, p):
        part = rows.at[q, core, yd if which else yu, p]
        return copy(part, part, y_s.at[q, which, p], y_r.at[q, which, p], up_y if which else down_y)

    def f_copy(q, which):
        part = rows.at[q, core, yd if which else yu, which]
        return copy(part, part, f_s.at[q, which], f_r.at[q, which], up_y if which else down_y)

    def f_arrived(q, which):
        part = rows.at[q, core, yo, which]
        return copy(part, part, f_s.at[q, which], f_r.at[q, which], up_y if which else down_y)

    def k_copy(q, dest, half):
        part = rows.at[q, half, dest]
        return copy(part, part, k_s.at[q, dest], k_r.at[q, dest], sibling)

    def z_copy(q, slot):
        return copy(zout.at[q, slot], zin.at[q, slot], z_s.at[q, slot], z_r.at[q, slot], down_z if slot in (2, 3, 5) else up_z)

    def o_copy(e):
        return copy(out16.at[e], in16.at[tile], o_s.at[e], o_r.at[tile], {"tile": e})

    def o_arrived(e):
        return copy(out16.at[e], in16.at[e], o_s.at[e], o_r.at[e], {"tile": e})

    barrier = pltpu.get_barrier_semaphore()

    def greet(e, _):
        @pl.when(e != tile)
        def _():
            pl.semaphore_signal(barrier, inc=1, device_id={"tile": e}, device_id_type=MESH)
        return 0

    for device in (partner, bridge, up_z, down_z):
        pl.semaphore_signal(barrier, inc=1, device_id=device, device_id_type=MESH)
    lax.fori_loop(0, 16, greet, 0)

    own = pltpu.make_async_copy(grad, cols.at[a], g_s)
    own.start()
    old_stats = pltpu.make_async_copy(stats_in, stats, t_s)
    old_stats.start()
    pl.semaphore_wait(barrier, 19)

    def begin(q, _):
        c_copy(q).start()
        return 0

    @pl.when(middle)
    def _():
        b_copy(0, 0).start()
    lax.fori_loop(0, Q, begin, 0)
    own.wait()

    def c_step(q):
        @pl.when(middle & (q > 0))
        def _():
            b_copy(q, 0).start()
        c_arrived(q).wait_recv()

        @pl.when(middle)
        def _():
            b_copy(q, 1).start()

    def ready(q, p, which):
        @pl.when(middle)
        def _():
            b_arrived(q, which).wait_recv()

        @pl.when(jnp.logical_not(middle))
        def _():
            rows[q, core, y, p] = cols[p, pl.ds(pl.multiple_of(q * high, high), high), :]

    def e1(q, which):
        p = jnp.where(middle, 1 - a, a)
        p = 1 - p if which else p
        ready(q, p, which)
        for way in range(2):
            y_copy(q, way, p).start()
        if which:
            k_copy(q, y, core).start()

    def e2(q):
        for which in range(2):
            y_arrived(q, which, which).wait_recv()
            f_copy(q, which).start()
        for which in range(2):
            y_arrived(q, which, 1 - which).wait_recv()
        for dest in (yu, yd):
            k_copy(q, dest, core).start()

    def e3(q):
        for which in range(2):
            f_arrived(q, which).wait_recv()
        k_copy(q, yo, core).start()

    def product(q, dest):
        k_copy(q, dest, 1 - core).wait_recv()
        total = None
        for p in range(2):
            right = jnp.concatenate([rows[q, half, dest, p] for half in range(2)], axis=0)
            part = lax.dot_general(cols[p], right, (((1,), (1,)), ((), ())), preferred_element_type=jnp.float32)
            total = part if total is None else total + part
        prod[q, dest] = total
        for slot, half, goal in ((4, 1, zo), (5, 0, zo), (0, 0, zu), (3, 1, zd)):
            @pl.when(dest == goal)
            def _(slot=slot, half=half):
                zout[q, slot] = pack(total[half * part_w:(half + 1) * part_w])
                z_copy(q, slot).start()

    def e4a(q):
        def one(k, _):
            product(q, jnp.where(k == 0, y, jnp.where(k == 1, yu, yd)))
            return 0

        lax.fori_loop(0, 3, one, 0)

    def e4b(q):
        product(q, yo)

    def e5(q):
        for slot, half, dest in ((1, 1, zu), (2, 0, zd)):
            z_copy(q, 3 + slot).wait_recv()
            zout[q, slot] = pack(prod[q, dest, half * part_w:(half + 1) * part_w, :] + unpack(zin[q, 3 + slot]))
            z_copy(q, slot).start()

    def e6(q):
        for slot in range(4):
            z_copy(q, slot).wait_recv()
        summed = prod[q, z] + jnp.concatenate([unpack(zin[q, k]) + unpack(zin[q, k + 2]) for k in range(2)], axis=0)
        lane = lax.broadcasted_iota(jnp.int32, (width, 2 * high), 1) // high
        places, shifts = [], []
        for half in range(2):
            at_ = half * Q + q
            places.append(pl.ds(pl.multiple_of(at_ // 2 * (2 * high), 2 * high), 2 * high))
            shifts.append((at_ + half) % 2 * high)
        old = [pltpu.roll(stats[:, places[half]], shifts[half], axis=1) for half in range(2)]
        fresh = EMA_DECAY * jnp.where(lane == 0, old[0], old[1]) + (1.0 - EMA_DECAY) * summed
        for half in range(2):
            moved = pltpu.roll(fresh, shifts[half], axis=1)
            refreshed[:, places[half]] = jnp.where(lane == (half * Q + q) % 2, moved, refreshed[:, places[half]])
        across = fresh.T
        pieces, powers = [], []
        for first in range(0, width, 128):
            part = across[:, first:min(first + 128, width)]
            whole, power = encode(part, 1)
            pieces.append(whole)
            powers.append(jnp.broadcast_to(power, (2 * high, 16)))
        code = jnp.concatenate(pieces + powers, axis=1).reshape(2, high // 8, 8, 512)
        for half in range(2):
            coded[pl.ds(half * (width // 8) + q * (high // 8), high // 8)] = code[half]

    def step(i, _):
        def at_step(first, fun):
            pl.when((i >= first) & (i < first + Q))(functools.partial(fun, i - first))

        at_step(0, functools.partial(e1, which=0))
        for k in range(2):
            pl.when(2 * i + k < Q)(functools.partial(c_step, 2 * i + k))
        at_step(0, functools.partial(e1, which=1))
        at_step(1, e2)
        pl.when(i == 3)(functools.partial(e4a, 0))
        pl.when(i == 3)(functools.partial(e4b, 0))
        pl.when((i >= 3) & (i < Q + 2))(functools.partial(e4a, i - 2))
        at_step(2, e3)
        pl.when((i >= 3) & (i < Q + 2))(functools.partial(e4b, i - 2))
        pl.when(i == 4)(functools.partial(e5, 0))
        pl.when((i >= 4) & (i < Q + 3))(functools.partial(e5, i - 3))
        pl.when(i == 4)(old_stats.wait)
        pl.when(i == 5)(functools.partial(e6, 0))
        pl.when((i >= 5) & (i < Q + 4))(functools.partial(e6, i - 4))
        return 0

    lax.fori_loop(0, Q + 4, step, 0)

    done = pltpu.make_async_copy(refreshed, refreshed_out, w_s)
    done.start()

    def peer(j):
        return (b + 1 - j // 8) % 2 * 8 + (y + 1 + j // 2) % 4 * 2 + (core + 1 - j % 2) % 2

    whole = width // 128 * 128

    def send(j, _):
        e = peer(j)
        count, first, second = jnp.int32(0), jnp.int32(0), jnp.int32(0)
        for u in range(16):
            mine = (owner[0, u] == e).astype(jnp.int32)
            first = first + jnp.where(count == 0, mine * u, 0)
            second = second + jnp.where(count == 1, mine * u, 0)
            count = count + mine
        pieces = []
        for s, u in enumerate((first, second)):
            held = (count > s).astype(jnp.float32)
            pieces += [coded[u * (unit // 8) + k] * held for k in range(unit // 8)]
        both = jnp.concatenate(pieces, axis=0)
        tail = jnp.concatenate([both[:unit, whole:width], both[unit:, whole:width]], axis=1)
        scales = jnp.concatenate([both[:, width:], jnp.zeros((128 - 2 * unit, 512 - width), jnp.float32)], axis=0).T
        scales = jnp.concatenate([scales[16 * k:16 * k + 1] for k in range(4)] + [jnp.zeros((4, 128), jnp.float32)], axis=0)
        tiles = [both[:, first:first + 128] for first in range(0, whole, 128)]
        out16[e] = jnp.concatenate(tiles + [tail, scales], axis=0).astype(jnp.int32).astype(jnp.int16)

        @pl.when(j < 15)
        def _():
            o_copy(e).start()
        return 0

    lax.fori_loop(0, 16, send, 0)

    kept = pltpu.make_async_copy(out16.at[tile], in16.at[tile], m_s)
    kept.start()

    def arrive(j, _):
        o_arrived(peer(j)).wait_recv()
        return 0

    lax.fori_loop(0, 15, arrive, 0)
    kept.wait()
    done.wait()

    def drain(q, _):
        c_copy(q).wait_send()

        @pl.when(middle)
        def _():
            for which in range(2):
                b_copy(q, which).wait_send()
        for which in range(2):
            for p in range(2):
                y_copy(q, which, p).wait_send()
            f_copy(q, which).wait_send()
        for dest in range(4):
            k_copy(q, dest, core).wait_send()
        for slot in range(6):
            z_copy(q, slot).wait_send()
        return 0

    lax.fori_loop(0, Q, drain, 0)

    def drain_owned(j, _):
        o_copy(peer(j)).wait_send()
        return 0

    lax.fori_loop(0, 15, drain_owned, 0)


def finish(refreshed, in16, refreshed_out, owned):
    refreshed_out[...] = refreshed[...]
    unit = owned.shape[1]
    tiles = 16 // STEPS
    width = owned.shape[2] // tiles
    parts = []
    count = width // 128
    for c in range(tiles):
        got = in16[c].astype(jnp.int32).astype(jnp.float32)
        tail = got[2 * unit * count:2 * unit * count + unit]
        scales = got[2 * unit * count + unit:]
        scales = step_of(jnp.concatenate([scales, jnp.zeros((128 - scales.shape[0], 128), jnp.float32)], axis=0).T)
        pieces = [got[2 * unit * k:2 * unit * (k + 1)] * scales[:2 * unit, k:k + 1] for k in range(count)]
        rest = width - 128 * count
        last = jnp.concatenate([tail[:, :rest], tail[:, rest:2 * rest]], axis=0)
        pieces.append(last * scales[:2 * unit, count:count + 1])
        parts.append(jnp.concatenate(pieces, axis=1))
    both = jnp.concatenate(parts, axis=1)
    for s in range(2):
        owned[s] = both[s * unit:(s + 1) * unit]


def local(gradient, stats_old, owner_map):
    depth, width = gradient.shape
    high = width // Q
    rows = stats_old.shape[0]
    unit = rows // 16
    dma = pltpu.SemaphoreType.DMA
    hbm = pl.BlockSpec(memory_space=pl.ANY)
    refreshed, in16 = pl.pallas_call(
        kernel,
        out_shape=(
            jax.ShapeDtypeStruct((width, rows), jnp.float32),
            jax.ShapeDtypeStruct((16, 2 * unit * (width // 128) + unit + 8, 128), jnp.int16),
        ),
        in_specs=[hbm, hbm, pl.BlockSpec(memory_space=pltpu.SMEM)],
        out_specs=(hbm, hbm),
        scratch_shapes=[
            pltpu.VMEM((2, width, depth), jnp.bfloat16),
            pltpu.VMEM((Q, 2, 4, 2, high, depth), jnp.bfloat16),
            pltpu.VMEM((width, rows), jnp.float32),
            pltpu.VMEM((width, rows), jnp.float32),
            pltpu.VMEM((Q, 4, width, 2 * high), jnp.float32),
            pltpu.VMEM((Q, 6, width // 2 + 16, 2 * high), jnp.int16),
            pltpu.VMEM((Q, 6, width // 2 + 16, 2 * high), jnp.int16),
            pltpu.VMEM((rows // 8, 8, 512), jnp.float32),
            pltpu.VMEM((16, 2 * unit * (width // 128) + unit + 8, 128), jnp.int16),
            dma, dma, dma, dma,
            dma((Q,)), dma((Q,)),
            dma((Q, 2)), dma((Q, 2)),
            dma((Q, 2, 2)), dma((Q, 2, 2)),
            dma((Q, 2)), dma((Q, 2)),
            dma((Q, 4)), dma((Q, 4)),
            dma((Q, 6)), dma((Q, 6)),
            dma((16,)), dma((16,)),
        ],
        compiler_params=pltpu.CompilerParams(
            collective_id=0, has_side_effects=True, vmem_limit_bytes=60 << 20
        ),
    )(gradient.T, stats_old.T, owner_map)
    refreshed, owned = pl.pallas_call(
        finish,
        grid=(STEPS,),
        out_shape=(
            jax.ShapeDtypeStruct((width, rows), jnp.float32),
            jax.ShapeDtypeStruct((2, unit, 16 * width), jnp.float32),
        ),
        in_specs=[
            pl.BlockSpec((width // STEPS, rows), lambda i: (i, 0)),
            pl.BlockSpec((16 // STEPS, 2 * unit * (width // 128) + unit + 8, 128), lambda i: (i, 0, 0)),
        ],
        out_specs=(
            pl.BlockSpec((width // STEPS, rows), lambda i: (i, 0)),
            pl.BlockSpec((2, unit, 16 // STEPS * width), lambda i: (0, 0, i)),
        ),
        compiler_params=pltpu.CompilerParams(vmem_limit_bytes=60 << 20),
    )(refreshed, in16)
    return refreshed.T, owned


def solution(mesh):
    return jax.shard_map(
        local,
        mesh=mesh,
        in_specs=(P("dp", "tile"), P("dp", "tile"), P("dp", None)),
        out_specs=(P("dp", "tile"), P(("dp", "tile"), None, None)),
        check_vma=False,
    )
```

```python
import functools

import jax
import jax.numpy as jnp
from jax import lax
from jax.experimental import pallas as pl
from jax.experimental.pallas import tpu as pltpu
from jax.sharding import PartitionSpec as P

MESH = pl.DeviceIdType.MESH
EMA_DECAY = 0.9
Q = 7
STEPS = 4
LEVELS = 32767.0


def encode(values, axis):
    most = jnp.maximum(jnp.max(jnp.abs(values), axis=axis, keepdims=True), 2.0 ** -100)
    power = jnp.ceil(8.0 * jnp.log2(most))
    return jnp.round(jnp.clip(values * jnp.exp2(15.0 - 0.125 * power), -LEVELS, LEVELS)), power


def step_of(power):
    return jnp.exp2(0.125 * power - 15.0)


def pack(values):
    whole, power = encode(values, 0)
    return jnp.concatenate([whole, jnp.broadcast_to(power, (16, power.shape[1]))], axis=0).astype(jnp.int32).astype(jnp.int16)


def unpack(code):
    high = code.shape[0] - 16
    code = code.astype(jnp.int32).astype(jnp.float32)
    return code[:high] * step_of(code[high:high + 1])


def kernel(grad, stats_in, owner, refreshed_out, in16, cols, rows, stats, refreshed, prod, zin, zout, coded, out16,
           g_s, t_s, w_s, m_s, c_s, c_r, b_s, b_r, y_s, y_r, f_s, f_r, k_s, k_r, z_s, z_r, o_s, o_r):
    width, depth = grad.shape
    high = width // Q
    part_w = width // 2
    unit = 8 * coded.shape[0] // 16
    dp, tile = lax.axis_index("dp"), lax.axis_index("tile")
    a, z = dp // 4, dp % 4
    b, y, core = tile // 8, (tile // 2) % 4, tile % 2
    middle = a != b

    def at(a_, z_, b_, y_, core_):
        return {"dp": a_ * 4 + z_, "tile": b_ * 8 + y_ * 2 + core_}

    partner = at(1 - a, z, b, y, core)
    bridge = at(1 - a, z, 1 - b, y, core)
    sibling = at(a, z, b, y, 1 - core)
    yu, yd, yo = (y + 1) % 4, (y + 3) % 4, (y + 2) % 4
    zu, zd, zo = (z + 1) % 4, (z + 3) % 4, (z + 2) % 4
    up_y, down_y = at(a, z, b, yu, core), at(a, z, b, yd, core)
    up_z, down_z = at(a, zu, b, y, core), at(a, zd, b, y, core)

    def copy(src, dst, send, recv, device):
        return pltpu.make_async_remote_copy(
            src_ref=src, dst_ref=dst, send_sem=send, recv_sem=recv, device_id=device, device_id_type=MESH
        )

    def c_copy(q):
        place = pl.ds(q * high, high)
        return copy(grad.at[place], cols.at[a, place], c_s.at[q], c_r.at[q], partner)

    def c_arrived(q):
        part = cols.at[1 - a, pl.ds(q * high, high)]
        return copy(part, part, c_s.at[q], c_r.at[q], partner)

    def b_copy(q, which):
        place = pl.ds(q * high, high)
        p = 1 - a if which else a
        return copy(cols.at[p, place] if which else grad.at[place], rows.at[q, core, y, p], b_s.at[q, which], b_r.at[q, which], bridge)

    def b_arrived(q, which):
        part = rows.at[q, core, y, a if which else 1 - a]
        return copy(part, part, b_s.at[q, which], b_r.at[q, which], bridge)

    def y_copy(q, which, p):
        part = rows.at[q, core, y, p]
        return copy(part, part, y_s.at[q, which, p], y_r.at[q, which, p], up_y if which else down_y)

    def y_arrived(q, which, p):
        part = rows.at[q, core, yd if which else yu, p]
        return copy(part, part, y_s.at[q, which, p], y_r.at[q, which, p], up_y if which else down_y)

    def f_copy(q, which):
        part = rows.at[q, core, yd if which else yu, which]
        return copy(part, part, f_s.at[q, which], f_r.at[q, which], up_y if which else down_y)

    def f_arrived(q, which):
        part = rows.at[q, core, yo, which]
        return copy(part, part, f_s.at[q, which], f_r.at[q, which], up_y if which else down_y)

    def k_copy(q, dest, half):
        part = rows.at[q, half, dest]
        return copy(part, part, k_s.at[q, dest], k_r.at[q, dest], sibling)

    def z_copy(q, slot):
        return copy(zout.at[q, slot], zin.at[q, slot], z_s.at[q, slot], z_r.at[q, slot], down_z if slot in (2, 3, 5) else up_z)

    def o_copy(e):
        return copy(out16.at[e], in16.at[tile], o_s.at[e], o_r.at[tile], {"tile": e})

    def o_arrived(e):
        return copy(out16.at[e], in16.at[e], o_s.at[e], o_r.at[e], {"tile": e})

    barrier = pltpu.get_barrier_semaphore()

    def greet(e, _):
        @pl.when(e != tile)
        def _():
            pl.semaphore_signal(barrier, inc=1, device_id={"tile": e}, device_id_type=MESH)
        return 0

    for device in (partner, bridge, up_z, down_z):
        pl.semaphore_signal(barrier, inc=1, device_id=device, device_id_type=MESH)
    lax.fori_loop(0, 16, greet, 0)

    own = pltpu.make_async_copy(grad, cols.at[a], g_s)
    own.start()
    old_stats = pltpu.make_async_copy(stats_in, stats, t_s)
    old_stats.start()
    pl.semaphore_wait(barrier, 19)

    def begin(q, _):
        c_copy(q).start()
        return 0

    @pl.when(middle)
    def _():
        b_copy(0, 0).start()
    lax.fori_loop(0, Q, begin, 0)
    own.wait()

    def c_step(q):
        @pl.when(middle & (q > 0))
        def _():
            b_copy(q, 0).start()
        c_arrived(q).wait_recv()

        @pl.when(middle)
        def _():
            b_copy(q, 1).start()

    def ready(q, p, which):
        @pl.when(middle)
        def _():
            b_arrived(q, which).wait_recv()

        @pl.when(jnp.logical_not(middle))
        def _():
            rows[q, core, y, p] = cols[p, pl.ds(pl.multiple_of(q * high, high), high), :]

    def e1(q, which):
        p = jnp.where(middle, 1 - a, a)
        p = 1 - p if which else p
        ready(q, p, which)
        for way in range(2):
            y_copy(q, way, p).start()
        if which:
            k_copy(q, y, core).start()

    def e2(q):
        for which in range(2):
            y_arrived(q, which, which).wait_recv()
            f_copy(q, which).start()
        for which in range(2):
            y_arrived(q, which, 1 - which).wait_recv()
        for dest in (yu, yd):
            k_copy(q, dest, core).start()

    def e3(q):
        for which in range(2):
            f_arrived(q, which).wait_recv()
        k_copy(q, yo, core).start()

    def product(q, dest):
        k_copy(q, dest, 1 - core).wait_recv()
        total = None
        for p in range(2):
            right = jnp.concatenate([rows[q, half, dest, p] for half in range(2)], axis=0)
            part = lax.dot_general(cols[p], right, (((1,), (1,)), ((), ())), preferred_element_type=jnp.float32)
            total = part if total is None else total + part
        prod[q, dest] = total
        for slot, half, goal in ((4, 1, zo), (5, 0, zo), (0, 0, zu), (3, 1, zd)):
            @pl.when(dest == goal)
            def _(slot=slot, half=half):
                zout[q, slot] = pack(total[half * part_w:(half + 1) * part_w])
                z_copy(q, slot).start()

    def e4a(q):
        def one(k, _):
            product(q, jnp.where(k == 0, y, jnp.where(k == 1, yu, yd)))
            return 0

        lax.fori_loop(0, 3, one, 0)

    def e4b(q):
        product(q, yo)

    def e5(q):
        for slot, half, dest in ((1, 1, zu), (2, 0, zd)):
            z_copy(q, 3 + slot).wait_recv()
            zout[q, slot] = pack(prod[q, dest, half * part_w:(half + 1) * part_w, :] + unpack(zin[q, 3 + slot]))
            z_copy(q, slot).start()

    def e6(q):
        for slot in range(4):
            z_copy(q, slot).wait_recv()
        summed = prod[q, z] + jnp.concatenate([unpack(zin[q, k]) + unpack(zin[q, k + 2]) for k in range(2)], axis=0)
        lane = lax.broadcasted_iota(jnp.int32, (width, 2 * high), 1) // high
        places, shifts = [], []
        for half in range(2):
            at_ = half * Q + q
            places.append(pl.ds(pl.multiple_of(at_ // 2 * (2 * high), 2 * high), 2 * high))
            shifts.append((at_ + half) % 2 * high)
        old = [pltpu.roll(stats[:, places[half]], shifts[half], axis=1) for half in range(2)]
        fresh = EMA_DECAY * jnp.where(lane == 0, old[0], old[1]) + (1.0 - EMA_DECAY) * summed
        for half in range(2):
            moved = pltpu.roll(fresh, shifts[half], axis=1)
            refreshed[:, places[half]] = jnp.where(lane == (half * Q + q) % 2, moved, refreshed[:, places[half]])
        across = fresh.T
        pieces, powers = [], []
        for first in range(0, width, 128):
            part = across[:, first:min(first + 128, width)]
            whole, power = encode(part, 1)
            pieces.append(whole)
            powers.append(jnp.broadcast_to(power, (2 * high, 16)))
        code = jnp.concatenate(pieces + powers, axis=1).reshape(2, high // 8, 8, 512)
        for half in range(2):
            coded[pl.ds(half * (width // 8) + q * (high // 8), high // 8)] = code[half]

    def step(i, _):
        def at_step(first, fun):
            pl.when((i >= first) & (i < first + Q))(functools.partial(fun, i - first))

        at_step(0, functools.partial(e1, which=0))
        for k in range(2):
            pl.when(2 * i + k < Q)(functools.partial(c_step, 2 * i + k))
        at_step(0, functools.partial(e1, which=1))
        at_step(1, e2)
        pl.when(i == 3)(functools.partial(e4a, 0))
        pl.when(i == 3)(functools.partial(e4b, 0))
        pl.when((i >= 3) & (i < Q + 2))(functools.partial(e4a, i - 2))
        at_step(2, e3)
        pl.when((i >= 3) & (i < Q + 2))(functools.partial(e4b, i - 2))
        pl.when(i == 4)(functools.partial(e5, 0))
        pl.when((i >= 4) & (i < Q + 3))(functools.partial(e5, i - 3))
        pl.when(i == 4)(old_stats.wait)
        pl.when(i == 5)(functools.partial(e6, 0))
        pl.when((i >= 5) & (i < Q + 4))(functools.partial(e6, i - 4))
        return 0

    lax.fori_loop(0, Q + 4, step, 0)

    done = pltpu.make_async_copy(refreshed, refreshed_out, w_s)
    done.start()

    def peer(j):
        return (b + 1 - j // 8) % 2 * 8 + (y + 1 + j // 2) % 4 * 2 + (core + 1 - j % 2) % 2

    whole = width // 128 * 128

    def send(j, _):
        e = peer(j)
        count, first, second = jnp.int32(0), jnp.int32(0), jnp.int32(0)
        for u in range(16):
            mine = (owner[0, u] == e).astype(jnp.int32)
            first = first + jnp.where(count == 0, mine * u, 0)
            second = second + jnp.where(count == 1, mine * u, 0)
            count = count + mine
        pieces = []
        for s, u in enumerate((first, second)):
            held = (count > s).astype(jnp.float32)
            pieces += [coded[u * (unit // 8) + k] * held for k in range(unit // 8)]
        both = jnp.concatenate(pieces, axis=0)
        tail = jnp.concatenate([both[:unit, whole:width], both[unit:, whole:width]], axis=1)
        scales = jnp.concatenate([both[:, width:], jnp.zeros((128 - 2 * unit, 512 - width), jnp.float32)], axis=0).T
        scales = jnp.concatenate([scales[16 * k:16 * k + 1] for k in range(4)] + [jnp.zeros((4, 128), jnp.float32)], axis=0)
        tiles = [both[:, first:first + 128] for first in range(0, whole, 128)]
        out16[e] = jnp.concatenate(tiles + [tail, scales], axis=0).astype(jnp.int32).astype(jnp.int16)

        @pl.when(j < 15)
        def _():
            o_copy(e).start()
        return 0

    lax.fori_loop(0, 16, send, 0)

    kept = pltpu.make_async_copy(out16.at[tile], in16.at[tile], m_s)
    kept.start()

    def arrive(j, _):
        o_arrived(peer(j)).wait_recv()
        return 0

    lax.fori_loop(0, 15, arrive, 0)
    kept.wait()
    done.wait()

    def drain(q, _):
        c_copy(q).wait_send()

        @pl.when(middle)
        def _():
            for which in range(2):
                b_copy(q, which).wait_send()
        for which in range(2):
            for p in range(2):
                y_copy(q, which, p).wait_send()
            f_copy(q, which).wait_send()
        for dest in range(4):
            k_copy(q, dest, core).wait_send()
        for slot in range(6):
            z_copy(q, slot).wait_send()
        return 0

    lax.fori_loop(0, Q, drain, 0)

    def drain_owned(j, _):
        o_copy(peer(j)).wait_send()
        return 0

    lax.fori_loop(0, 15, drain_owned, 0)


def finish(refreshed, in16, refreshed_out, owned):
    refreshed_out[...] = refreshed[...]
    unit = owned.shape[1]
    tiles = 16 // STEPS
    width = owned.shape[2] // tiles
    parts = []
    count = width // 128
    for c in range(tiles):
        got = in16[c].astype(jnp.int32).astype(jnp.float32)
        tail = got[2 * unit * count:2 * unit * count + unit]
        scales = got[2 * unit * count + unit:]
        scales = step_of(jnp.concatenate([scales, jnp.zeros((128 - scales.shape[0], 128), jnp.float32)], axis=0).T)
        pieces = [got[2 * unit * k:2 * unit * (k + 1)] * scales[:2 * unit, k:k + 1] for k in range(count)]
        rest = width - 128 * count
        last = jnp.concatenate([tail[:, :rest], tail[:, rest:2 * rest]], axis=0)
        pieces.append(last * scales[:2 * unit, count:count + 1])
        parts.append(jnp.concatenate(pieces, axis=1))
    both = jnp.concatenate(parts, axis=1)
    for s in range(2):
        owned[s] = both[s * unit:(s + 1) * unit]


def local(gradient, stats_old, owner_map):
    depth, width = gradient.shape
    high = width // Q
    rows = stats_old.shape[0]
    unit = rows // 16
    dma = pltpu.SemaphoreType.DMA
    hbm = pl.BlockSpec(memory_space=pl.ANY)
    refreshed, in16 = pl.pallas_call(
        kernel,
        out_shape=(
            jax.ShapeDtypeStruct((width, rows), jnp.float32),
            jax.ShapeDtypeStruct((16, 2 * unit * (width // 128) + unit + 8, 128), jnp.int16),
        ),
        in_specs=[hbm, hbm, pl.BlockSpec(memory_space=pltpu.SMEM)],
        out_specs=(hbm, hbm),
        scratch_shapes=[
            pltpu.VMEM((2, width, depth), jnp.bfloat16),
            pltpu.VMEM((Q, 2, 4, 2, high, depth), jnp.bfloat16),
            pltpu.VMEM((width, rows), jnp.float32),
            pltpu.VMEM((width, rows), jnp.float32),
            pltpu.VMEM((Q, 4, width, 2 * high), jnp.float32),
            pltpu.VMEM((Q, 6, width // 2 + 16, 2 * high), jnp.int16),
            pltpu.VMEM((Q, 6, width // 2 + 16, 2 * high), jnp.int16),
            pltpu.VMEM((rows // 8, 8, 512), jnp.float32),
            pltpu.VMEM((16, 2 * unit * (width // 128) + unit + 8, 128), jnp.int16),
            dma, dma, dma, dma,
            dma((Q,)), dma((Q,)),
            dma((Q, 2)), dma((Q, 2)),
            dma((Q, 2, 2)), dma((Q, 2, 2)),
            dma((Q, 2)), dma((Q, 2)),
            dma((Q, 4)), dma((Q, 4)),
            dma((Q, 6)), dma((Q, 6)),
            dma((16,)), dma((16,)),
        ],
        compiler_params=pltpu.CompilerParams(
            collective_id=0, has_side_effects=True, vmem_limit_bytes=60 << 20
        ),
    )(gradient.T, stats_old.T, owner_map)
    refreshed, owned = pl.pallas_call(
        finish,
        grid=(STEPS,),
        out_shape=(
            jax.ShapeDtypeStruct((width, rows), jnp.float32),
            jax.ShapeDtypeStruct((2, unit, 16 * width), jnp.float32),
        ),
        in_specs=[
            pl.BlockSpec((width // STEPS, rows), lambda i: (i, 0)),
            pl.BlockSpec((16 // STEPS, 2 * unit * (width // 128) + unit + 8, 128), lambda i: (i, 0, 0)),
        ],
        out_specs=(
            pl.BlockSpec((width // STEPS, rows), lambda i: (i, 0)),
            pl.BlockSpec((2, unit, 16 // STEPS * width), lambda i: (0, 0, i)),
        ),
        compiler_params=pltpu.CompilerParams(vmem_limit_bytes=60 << 20),
    )(refreshed, in16)
    return refreshed.T, owned


def solution(mesh):
    return jax.shard_map(
        local,
        mesh=mesh,
        in_specs=(P("dp", "tile"), P("dp", "tile"), P("dp", None)),
        out_specs=(P("dp", "tile"), P(("dp", "tile"), None, None)),
        check_vma=False,
    )
```
